32 devices in a mesh: groups: 2 (over y), pfx: 4 (over z), smp: 2 (over x), kv: 2 (over core).
Axes of the slice: x: 2, y: 2, z: 4, core: 2. Of those that a mesh axis runs over, the one named last changes fastest.
Arguments:
- hidden: bfloat16 [64, 8192], P(('groups', 'smp'), 'pfx'), parts along dimension 0, may hold values from -6 to 6
- norm_gain: bfloat16 [8192], P('pfx'), may hold values from 0.5 to 1.5
- query_weight: bfloat16 [8192, 4096], P('pfx', 'kv'), may hold values from -0.0625 to 0.0625
- key_matrix: bfloat16 [8192, 512], P('pfx', 'kv'), may hold values from -0.52734375 to 0.52734375
- value_matrix: bfloat16 [8192, 512], P('pfx', 'kv'), may hold values from -0.0625 to 0.0625
- prefix_key: bfloat16 [16384, 512], P(('groups', 'pfx', 'smp'), 'kv'), parts along dimension 0, may hold values from -160 to 160
- shared_prefix_value: bfloat16 [16384, 512], P(('groups', 'pfx', 'smp'), 'kv'), parts along dimension 0, may hold values from -6 to 6
- sample_suffix_key: bfloat16 [64, 128, 512], P(('groups', 'smp'), 'pfx', 'kv'), parts along dimension 0, may hold values from -24 to 24
- sample_suffix_value: bfloat16 [64, 128, 512], P(('groups', 'smp'), 'pfx', 'kv'), parts along dimension 0, may hold values from -6 to 6
- lengths: int32 [64], P(('groups', 'smp')), parts along dimension 0, may hold values from 1 to 128, as said below
- assign: int32 [64], P(('groups', 'smp')), parts along dimension 0, may hold values from 0 to 31, as said below
Outputs:
- attended: bfloat16 [64, 4096], P(('groups', 'smp'), 'kv'), parts along dimension 0
The draws below stay inside these ranges and needn't reach their ends.
There are 2 independent parts, one for each index of `groups`. The reference program is written for one: setup_inputs(seed, part) draws one part's arguments, and reference() takes and returns one part's arrays. A program takes and returns all parts, laid end to end along the dimension named above; an argument that names none is the same for every part. Nothing has to cross between parts.
Inputs may be any that keep to these rules, and one draw needn't show every extreme that they name: `lengths`: some sample has exactly 128 live positions. `assign`: each aligned block of 16 rows holds each sample number of that block once.
All inputs are finite; a program needn't handle non-finite values.
Results may differ from the reference program's by a relative error of at most 0.017.
Values may be sent and summed in bfloat16 or wider, within the bound.
A program may use at most 64 MiB of HBM per device.

```python
import jax
import jax.numpy as jnp
from jax import lax

MODEL_WIDTH = 8192
HEAD_WIDTH = 128
QUERY_HEADS = 32
KEY_VALUE_HEADS = 4
B_DEV = 16
SAMPLE_TOTAL = 32
PREFIX_LENGTH = 8192
SUFFIX_LENGTH = 128


def draw_prefix_key(key, part):
    starting_keys = jnp.clip(3.0 * jax.random.normal(key, (PREFIX_LENGTH, KEY_VALUE_HEADS * HEAD_WIDTH), jnp.float32), -48.0, 48.0)
    return starting_keys.astype(jnp.bfloat16)


def draw_lengths(key, part):
    length_draw = jax.random.randint(key, (SAMPLE_TOTAL,), 1, SUFFIX_LENGTH + 1)
    spot_index = jax.random.randint(jax.random.fold_in(key, 21), (), 0, SAMPLE_TOTAL)
    return length_draw.at[spot_index].set(SUFFIX_LENGTH).astype(jnp.int32)


def draw_assign(key, part):
    block_count = SAMPLE_TOTAL // B_DEV
    block_keys = jax.random.split(key, block_count)
    block_orders = jax.vmap(lambda block_key: jax.random.permutation(block_key, B_DEV))(block_keys)
    offsets = jnp.arange(block_count, dtype=jnp.int32)[:, None] * B_DEV
    return (block_orders.astype(jnp.int32) + offsets).reshape(SAMPLE_TOTAL)


def block_scale(key, shape, cuts, smallest, largest):
    gain = 1.0
    for dim, blocks in cuts:
        steps = jax.random.uniform(jax.random.fold_in(jax.random.fold_in(key, 6), dim), (blocks,), jnp.float32, smallest / len(cuts), largest / len(cuts))
        gain = gain * jnp.repeat(jnp.exp(steps), shape[dim] // blocks).reshape((-1,) + (1,) * (len(shape) - 1 - dim))
    return gain


def normal_values(key, shape, scale, reach, shards=(), kind=jnp.bfloat16):
    drawn = jax.random.normal(key, shape, jnp.float32) * scale
    if len(shards) > 0:
        drawn = block_scale(key, shape, shards, -0.22, 0.18) * drawn
    return jnp.clip(drawn, min=-reach, max=reach).astype(kind)


def setup_inputs(seed: int = 0, part: int = 0) -> dict:
    key_of = jax.random.split(jax.random.key(seed), 12)
    part_keys = jax.random.split(jax.random.fold_in(key_of[11], part), 12)
    hidden = normal_values(part_keys[0], (SAMPLE_TOTAL, MODEL_WIDTH), 1.0, 6.0, ((0, 2), (1, 4)))
    norm_gain = jnp.clip(1.0 + 0.1 * jax.random.normal(key_of[1], (MODEL_WIDTH,), jnp.float32), 0.5, 1.5).astype(jnp.bfloat16)
    query_weight = normal_values(key_of[2], (MODEL_WIDTH, QUERY_HEADS * HEAD_WIDTH), MODEL_WIDTH ** -0.5, 0.0625, ((0, 4), (1, 2)))
    key_matrix = normal_values(key_of[3], (MODEL_WIDTH, KEY_VALUE_HEADS * HEAD_WIDTH), (8.0 / MODEL_WIDTH ** 0.5), 0.52734375, ((0, 4), (1, 2)))
    value_matrix = normal_values(key_of[4], (MODEL_WIDTH, KEY_VALUE_HEADS * HEAD_WIDTH), MODEL_WIDTH ** -0.5, 0.0625, ((0, 4), (1, 2)))
    prefix_key = draw_prefix_key(jax.random.fold_in(jax.random.fold_in(key_of[11], part), 71), part)
    shared_prefix_value = normal_values(part_keys[6], (PREFIX_LENGTH, KEY_VALUE_HEADS * HEAD_WIDTH), 1.0, 6.0, ((0, 8), (1, 2)))
    sample_suffix_key = normal_values(part_keys[7], (SAMPLE_TOTAL, SUFFIX_LENGTH, KEY_VALUE_HEADS * HEAD_WIDTH), 4.0, 24.0, ((0, 2), (1, 4), (2, 2)))
    sample_suffix_value = normal_values(part_keys[8], (SAMPLE_TOTAL, SUFFIX_LENGTH, KEY_VALUE_HEADS * HEAD_WIDTH), 1.0, 6.0, ((0, 2), (1, 4), (2, 2)))
    lengths = draw_lengths(jax.random.fold_in(jax.random.fold_in(key_of[11], part), 71), part)
    assign = draw_assign(jax.random.fold_in(jax.random.fold_in(key_of[11], part), 71), part)
    return dict(hidden=hidden, norm_gain=norm_gain, query_weight=query_weight, key_matrix=key_matrix, value_matrix=value_matrix, prefix_key=prefix_key, shared_prefix_value=shared_prefix_value, sample_suffix_key=sample_suffix_key, sample_suffix_value=sample_suffix_value, lengths=lengths, assign=assign)


norm_eps = 1e-05
very_negative = -1e+30

def project(normed, weight, rms_value):
    product = jnp.dot(normed, weight, preferred_element_type=jnp.float32)
    return (product / rms_value[:, None]).astype(jnp.bfloat16)

def reference(hidden, norm_gain, query_weight, key_matrix, value_matrix, prefix_key, shared_prefix_value, sample_suffix_key, sample_suffix_value, lengths, assign):
    hidden_wide = hidden.astype(jnp.float32)
    rms_value = jnp.sqrt(lax.optimization_barrier(jnp.sum(hidden_wide * hidden_wide, axis=1)) / MODEL_WIDTH + norm_eps)
    normed = (hidden_wide * norm_gain.astype(jnp.float32)).astype(jnp.bfloat16)
    query_rows = project(normed, query_weight, rms_value)
    new_key = project(normed, key_matrix, rms_value)
    new_value = project(normed, value_matrix, rms_value)
    slot_length = jnp.take(lengths, assign, axis=0)
    slot_keys = jnp.take(sample_suffix_key, assign, axis=0)
    slot_values = jnp.take(sample_suffix_value, assign, axis=0)
    live_mask = jnp.arange(SUFFIX_LENGTH, dtype=jnp.int32)[None, :] < slot_length[:, None]
    group_width = QUERY_HEADS // KEY_VALUE_HEADS
    score_scale = HEAD_WIDTH ** (-0.5)

    def one_head(head_index):
        group_index = head_index // group_width
        head_query = lax.dynamic_slice_in_dim(query_rows, head_index * HEAD_WIDTH, HEAD_WIDTH, 1)
        prefix_keys = lax.dynamic_slice_in_dim(prefix_key, group_index * HEAD_WIDTH, HEAD_WIDTH, 1)
        prefix_values = lax.dynamic_slice_in_dim(shared_prefix_value, group_index * HEAD_WIDTH, HEAD_WIDTH, 1)
        suffix_keys = lax.dynamic_slice_in_dim(slot_keys, group_index * HEAD_WIDTH, HEAD_WIDTH, 2).astype(jnp.float32)
        suffix_values = lax.dynamic_slice_in_dim(slot_values, group_index * HEAD_WIDTH, HEAD_WIDTH, 2).astype(jnp.float32)
        own_key = lax.dynamic_slice_in_dim(new_key, group_index * HEAD_WIDTH, HEAD_WIDTH, 1).astype(jnp.float32)
        own_value = lax.dynamic_slice_in_dim(new_value, group_index * HEAD_WIDTH, HEAD_WIDTH, 1).astype(jnp.float32)
        query_wide = head_query.astype(jnp.float32)
        prefix_scores = jnp.dot(head_query, prefix_keys.T, preferred_element_type=jnp.float32) * score_scale
        suffix_scores = jnp.einsum('bd,bsd->bs', query_wide, suffix_keys, precision=lax.Precision.HIGHEST) * score_scale
        suffix_scores = jnp.where(live_mask, suffix_scores, very_negative)
        own_score = lax.optimization_barrier(jnp.sum(query_wide * own_key, axis=1)) * score_scale
        top_score = jnp.maximum(jnp.maximum(lax.optimization_barrier(jnp.max(prefix_scores, axis=1)), lax.optimization_barrier(jnp.max(suffix_scores, axis=1))), own_score)
        prefix_weights = jnp.exp(prefix_scores - top_score[:, None]).astype(jnp.bfloat16)
        suffix_weights = jnp.where(live_mask, jnp.exp(suffix_scores - top_score[:, None]), 0.0).astype(jnp.bfloat16)
        own_weight = lax.optimization_barrier(jnp.exp(own_score - top_score).astype(jnp.bfloat16)).astype(jnp.float32)
        denominator = lax.optimization_barrier(jnp.sum(prefix_weights.astype(jnp.float32), axis=1)) + lax.optimization_barrier(jnp.sum(suffix_weights.astype(jnp.float32), axis=1)) + own_weight
        numerator = jnp.dot(prefix_weights, prefix_values, preferred_element_type=jnp.float32)
        numerator = numerator + jnp.einsum('bs,bsd->bd', suffix_weights.astype(jnp.float32), suffix_values, precision=lax.Precision.HIGHEST)
        numerator = numerator + own_weight[:, None] * own_value
        return (numerator / denominator[:, None]).astype(jnp.bfloat16)
    heads = lax.map(one_head, jnp.arange(QUERY_HEADS, dtype=jnp.int32))
    return jnp.transpose(heads, (1, 0, 2)).reshape(SAMPLE_TOTAL, QUERY_HEADS * HEAD_WIDTH)
```

```python
import functools
import math

import jax
import jax.numpy as jnp
from jax import lax
from jax.experimental import pallas as pl
from jax.experimental.pallas import tpu as pltpu
from jax.sharding import PartitionSpec as P

MODEL_WIDTH = 8192
HEAD_WIDTH = 128


norm_eps = 1e-05
very_negative = -1e30


def prefix_head(operands):
    query_block, key_block, value_block = operands
    scores = jnp.einsum(
        "bgd,kd->bgk", query_block, key_block, preferred_element_type=jnp.float32
    ) * HEAD_WIDTH ** (-0.5)
    top_score = jnp.max(scores, axis=2)
    weights = jnp.exp(scores - top_score[..., None]).astype(jnp.bfloat16)
    denominator = jnp.sum(weights.astype(jnp.float32), axis=2)
    numerator = jnp.einsum("bgk,kd->bgd", weights, value_block, preferred_element_type=jnp.float32)
    return (numerator, denominator, top_score)


def plain_body(
    hidden,
    norm_gain,
    query_weight,
    key_matrix,
    value_matrix,
    prefix_key,
    shared_prefix_value,
    sample_suffix_key,
    sample_suffix_value,
    lengths,
    assign,
):
    local_rows = hidden.shape[0]
    local_kv = key_matrix.shape[1] // HEAD_WIDTH
    local_heads = query_weight.shape[1] // HEAD_WIDTH
    group_width = local_heads // local_kv
    score_scale = HEAD_WIDTH ** (-0.5)
    hidden_wide = hidden.astype(jnp.float32)
    normed = (hidden_wide * norm_gain.astype(jnp.float32)).astype(jnp.bfloat16)
    query_part = jnp.dot(normed, query_weight, preferred_element_type=jnp.float32)
    key_part = jnp.dot(normed, key_matrix, preferred_element_type=jnp.float32)
    value_part = jnp.dot(normed, value_matrix, preferred_element_type=jnp.float32)
    square_part = jnp.sum(hidden_wide * hidden_wide, axis=1)
    query_sum, key_sum, value_sum, square_sum = lax.psum(
        (query_part, key_part, value_part, square_part), "pfx"
    )
    rms_value = jnp.sqrt(square_sum / MODEL_WIDTH + norm_eps)
    query_rows = (query_sum / rms_value[:, None]).astype(jnp.bfloat16)
    new_key = (key_sum / rms_value[:, None]).astype(jnp.bfloat16)
    new_value = (value_sum / rms_value[:, None]).astype(jnp.bfloat16)
    all_queries = lax.all_gather(query_rows, "smp", axis=0, tiled=True)
    sample_count = all_queries.shape[0]
    head_queries = jnp.transpose(
        all_queries.reshape(sample_count, local_kv, group_width, HEAD_WIDTH), (1, 0, 2, 3)
    )
    head_keys = jnp.transpose(prefix_key.reshape(-1, local_kv, HEAD_WIDTH), (1, 0, 2))
    head_values = jnp.transpose(shared_prefix_value.reshape(-1, local_kv, HEAD_WIDTH), (1, 0, 2))
    pre_numer, pre_denom, pre_top = lax.map(prefix_head, (head_queries, head_keys, head_values))
    pre_numer = jnp.transpose(pre_numer, (1, 0, 2, 3)).reshape(
        sample_count, local_heads, HEAD_WIDTH
    )
    pre_denom = jnp.transpose(pre_denom, (1, 0, 2)).reshape(sample_count, local_heads)
    pre_top = jnp.transpose(pre_top, (1, 0, 2)).reshape(sample_count, local_heads)
    row_base = lax.axis_index("smp") * local_rows
    slot_index = assign - row_base
    one_hot = (slot_index[:, None] == jnp.arange(local_rows, dtype=jnp.int32)[None, :]).astype(
        jnp.float32
    )
    slot_query = jnp.einsum(
        "rs,rx->sx", one_hot, query_rows.astype(jnp.float32), precision=lax.Precision.HIGHEST
    ).astype(jnp.bfloat16)
    slot_query = slot_query.reshape(local_rows, local_kv, group_width, HEAD_WIDTH)
    suffix_len = sample_suffix_key.shape[1]
    suffix_keys = sample_suffix_key.reshape(local_rows, suffix_len, local_kv, HEAD_WIDTH)
    suffix_values = sample_suffix_value.reshape(local_rows, suffix_len, local_kv, HEAD_WIDTH)
    suffix_scores = (
        jnp.einsum("shgd,sthd->shgt", slot_query, suffix_keys, preferred_element_type=jnp.float32)
        * score_scale
    )
    position = lax.axis_index("pfx") * suffix_len + jnp.arange(suffix_len, dtype=jnp.int32)
    live_mask = (position[None, :] < lengths[:, None])[:, None, None, :]
    suffix_scores = jnp.where(live_mask, suffix_scores, very_negative)
    suffix_top = jnp.max(suffix_scores, axis=3)
    suffix_weights = jnp.where(
        live_mask, jnp.exp(suffix_scores - suffix_top[..., None]), 0.0
    ).astype(jnp.bfloat16)
    suffix_denom = jnp.sum(suffix_weights.astype(jnp.float32), axis=3)
    suffix_numer = jnp.einsum(
        "shgt,sthd->shgd", suffix_weights, suffix_values, preferred_element_type=jnp.float32
    )
    row_numer = jnp.einsum(
        "rs,shgd->rhgd", one_hot, suffix_numer, precision=lax.Precision.HIGHEST
    ).reshape(local_rows, local_heads, HEAD_WIDTH)
    row_denom = jnp.einsum(
        "rs,shg->rhg", one_hot, suffix_denom, precision=lax.Precision.HIGHEST
    ).reshape(local_rows, local_heads)
    row_top = jnp.einsum(
        "rs,shg->rhg", one_hot, suffix_top, precision=lax.Precision.HIGHEST
    ).reshape(local_rows, local_heads)
    full_top = lax.dynamic_update_slice(
        jnp.full((sample_count, local_heads), very_negative, jnp.float32), row_top, (row_base, 0)
    )
    local_top = jnp.maximum(pre_top, full_top)
    global_top = lax.pmax(local_top, ("pfx", "smp"))
    own_top = lax.dynamic_slice_in_dim(global_top, row_base, local_rows, 0)
    pre_factor = jnp.exp(pre_top - global_top)
    row_factor = jnp.exp(row_top - own_top)
    scaled_row_numer = row_numer * row_factor[..., None]
    scaled_row_denom = row_denom * row_factor
    term_numer = pre_numer * pre_factor[..., None]
    term_denom = pre_denom * pre_factor
    term_numer = lax.dynamic_update_slice(
        term_numer,
        lax.dynamic_slice_in_dim(term_numer, row_base, local_rows, 0) + scaled_row_numer,
        (row_base, 0, 0),
    )
    term_denom = lax.dynamic_update_slice(
        term_denom,
        lax.dynamic_slice_in_dim(term_denom, row_base, local_rows, 0) + scaled_row_denom,
        (row_base, 0),
    )
    block_numer, block_denom = (
        lax.psum_scatter(
            term_numer.astype(jnp.bfloat16), "smp", scatter_dimension=0, tiled=True
        ).astype(jnp.float32),
        lax.psum_scatter(
            term_denom.astype(jnp.bfloat16), "smp", scatter_dimension=0, tiled=True
        ).astype(jnp.float32),
    )
    numerator, denominator = (
        lax.psum(block_numer.astype(jnp.bfloat16), "pfx").astype(jnp.float32),
        lax.psum(block_denom.astype(jnp.bfloat16), "pfx").astype(jnp.float32),
    )
    query_wide = query_rows.reshape(local_rows, local_kv, group_width, HEAD_WIDTH).astype(
        jnp.float32
    )
    own_key = new_key.reshape(local_rows, local_kv, 1, HEAD_WIDTH).astype(jnp.float32)
    own_score = (jnp.sum(query_wide * own_key, axis=3) * score_scale).reshape(
        local_rows, local_heads
    )
    final_top = jnp.maximum(own_top, own_score)
    old_factor = jnp.exp(own_top - final_top)
    own_weight = lax.optimization_barrier(
        jnp.exp(own_score - final_top).astype(jnp.bfloat16)
    ).astype(jnp.float32)
    own_value = jnp.broadcast_to(
        new_value.reshape(local_rows, local_kv, 1, HEAD_WIDTH).astype(jnp.float32),
        (local_rows, local_kv, group_width, HEAD_WIDTH),
    ).reshape(local_rows, local_heads, HEAD_WIDTH)
    numerator = numerator * old_factor[..., None] + own_weight[..., None] * own_value
    denominator = denominator * old_factor + own_weight
    return (
        (numerator / denominator[..., None])
        .astype(jnp.bfloat16)
        .reshape(local_rows, local_heads * HEAD_WIDTH)
    )


def group_kernel(
    pfx,
    smp,
    hidden_hbm,
    gain_ref,
    query_weight_hbm,
    key_matrix_hbm,
    value_matrix_hbm,
    prefix_key_hbm,
    prefix_value_hbm,
    suffix_key_hbm,
    suffix_value_hbm,
    lengths_ref,
    assign_ref,
    out_ref,
    hidden_v,
    normed_v,
    query_weight_v,
    new_weight_v,
    keys_v,
    values_v,
    flipped_v,
    bias_v,
    square_v,
    query_part,
    query_recv,
    new_part,
    new_recv,
    queries_v,
    numer_send,
    stat_send,
    numer_recv,
    stat_recv,
    column_v,
    out_v,
    load_sem,
    square_sems,
    query_sems,
    new_sems,
    gather_sems,
    numer_sems,
    stat_sems,
    out_sems,
):
    rows, width = hidden_v.shape
    kv_heads, key_count, _ = keys_v.shape
    prefix_count = prefix_key_hbm.shape[0]
    suffix_count = suffix_key_hbm.shape[0]
    suffix_len = suffix_count // rows
    piece_cols = query_weight_v.shape[2]
    piece_heads = piece_cols // HEAD_WIDTH
    piece_rows = piece_heads * rows
    lanes = smp * piece_rows
    pieces_per_kv = pfx // kv_heads
    sources = pfx * smp
    power_scale = HEAD_WIDTH ** (-0.5) * math.log2(math.e)

    p = lax.axis_index("pfx")
    s = lax.axis_index("smp")
    me = p * smp + s

    def other_p(step):
        return lax.rem(p + step, pfx)

    def other_s(step):
        return lax.rem(s + step, smp)

    steps = sorted(range(1, pfx), key=lambda step: -min(step, pfx - step))
    order = steps + [0]
    peers = [(a, b) for a in [0] + steps for b in range(smp) if (a, b) != (0, 0)]

    def remote(source, target, sems, send_index, recv_index, to_p, to_s):
        return pltpu.make_async_remote_copy(
            src_ref=source,
            dst_ref=target,
            send_sem=sems.at[0, send_index],
            recv_sem=sems.at[1, recv_index],
            device_id={"pfx": to_p, "smp": to_s},
            device_id_type=pl.DeviceIdType.MESH,
        )

    loads = []

    def load(source, target):
        copy = pltpu.make_async_copy(source, target, load_sem.at[len(loads)])
        copy.start()
        loads.append(copy)
        return copy

    hidden_load = load(hidden_hbm, hidden_v)
    query_loads = []
    for slot, step in enumerate(order):
        start = pl.multiple_of(other_p(step) * piece_cols, piece_cols)
        query_loads.append(
            load(query_weight_hbm.at[:, pl.ds(start, piece_cols)], query_weight_v.at[slot])
        )
    new_loads = [
        load(key_matrix_hbm, new_weight_v.at[0]),
        load(value_matrix_hbm, new_weight_v.at[1]),
    ]
    value_loads, key_loads = [], []
    for g in range(kv_heads):
        head = pl.ds(g * HEAD_WIDTH, HEAD_WIDTH)
        early, late = pl.ds(0, prefix_count), pl.ds(prefix_count, suffix_count)
        value_loads.append(load(prefix_value_hbm.at[:, head], values_v.at[g, early]))
        value_loads.append(load(suffix_value_hbm.at[:, head], values_v.at[g, late]))
        key_loads.append(load(prefix_key_hbm.at[:, head], keys_v.at[g, early]))
        key_loads.append(load(suffix_key_hbm.at[:, head], keys_v.at[g, late]))

    barrier = pltpu.get_barrier_semaphore()
    for a, b in peers:
        pl.semaphore_signal(
            barrier,
            inc=1,
            device_id={"pfx": other_p(a), "smp": other_s(b)},
            device_id_type=pl.DeviceIdType.MESH,
        )

    hidden_load.wait()
    hidden_wide = hidden_v[...].astype(jnp.float32)
    normed_v[...] = (hidden_wide * gain_ref[...]).astype(jnp.bfloat16)
    square_part = jnp.sum(hidden_wide * hidden_wide, axis=1, keepdims=True)
    square_v[p] = jnp.broadcast_to(square_part, (rows, HEAD_WIDTH))
    pl.semaphore_wait(barrier, len(peers))

    sends = []
    for step in steps:
        copy = remote(square_v.at[p], square_v.at[p], square_sems, step, p, other_p(step), s)
        copy.start()
        sends.append(copy)

    for slot, step in enumerate(order):
        query_loads[slot].wait()
        query_part[slot] = jnp.dot(
            normed_v[...], query_weight_v[slot], preferred_element_type=jnp.float32
        )
        if step:
            copy = remote(
                query_part.at[slot], query_recv.at[p], query_sems, step, p, other_p(step), s
            )
            copy.start()
            sends.append(copy)
    for which in range(2):
        new_loads[which].wait()
        product = jnp.dot(
            normed_v[...], new_weight_v[which], preferred_element_type=jnp.float32
        )
        for g in range(kv_heads):
            new_part[g, :, which * HEAD_WIDTH : (which + 1) * HEAD_WIDTH] = product[
                :, g * HEAD_WIDTH : (g + 1) * HEAD_WIDTH
            ]
    for step in steps:
        copy = remote(
            new_part.at[other_p(step) // pieces_per_kv],
            new_recv.at[p],
            new_sems,
            step,
            p,
            other_p(step),
            s,
        )
        copy.start()
        sends.append(copy)

    ones = jnp.ones((flipped_v.shape[1] - HEAD_WIDTH, key_count), jnp.bfloat16)

    def eye(size):
        return (
            lax.broadcasted_iota(jnp.int32, (size, size), 0)
            == lax.broadcasted_iota(jnp.int32, (size, size), 1)
        ).astype(jnp.bfloat16)

    by_last = (((1,), (1,)), ((), ()))
    for copy in value_loads:
        copy.wait()
    for g in range(kv_heads):
        flipped_v[g, :HEAD_WIDTH, :] = lax.dot_general(
            eye(HEAD_WIDTH), values_v[g], by_last, preferred_element_type=jnp.float32
        ).astype(jnp.bfloat16)
        flipped_v[g, HEAD_WIDTH:, :] = ones
    lane = lax.broadcasted_iota(jnp.int32, (suffix_len, lanes), 1)
    position = lax.broadcasted_iota(jnp.int32, (suffix_len, lanes), 0) + p * suffix_len
    lane_row = lax.rem(lane, rows)
    lane_sample = jnp.full((suffix_len, lanes), -1, jnp.int32)
    for row in range(rows):
        lane_sample = jnp.where(lane_row == row, assign_ref[row] - s * rows, lane_sample)
    own_lane = (lane >= s * piece_rows) & (lane < (s + 1) * piece_rows)
    lane_sample = jnp.where(own_lane, lane_sample, -1)
    for sample in range(rows):
        live = (lane_sample == sample) & (position < lengths_ref[sample])
        bias_v[sample * suffix_len : (sample + 1) * suffix_len, :] = jnp.where(
            live, 0.0, very_negative
        )

    square_sum = square_v[p]
    query_sum = query_part[len(steps)]
    for step in steps:
        source = other_p(step)
        remote(square_v.at[p], square_v.at[source], square_sems, step, source, source, s).wait_recv()
        remote(
            query_part.at[0], query_recv.at[source], query_sems, step, source, source, s
        ).wait_recv()
        square_sum = square_sum + square_v[source]
        query_sum = query_sum + query_recv[source]
    rms_value = jnp.sqrt(square_sum / (width * pfx) + norm_eps)
    own_rows = pl.ds(pl.multiple_of(s * piece_rows, piece_rows), piece_rows)
    own_query = jnp.concatenate(
        [
            query_sum[:, h * HEAD_WIDTH : (h + 1) * HEAD_WIDTH] / rms_value
            for h in range(piece_heads)
        ],
        axis=0,
    ).astype(jnp.bfloat16)
    queries_v[p, own_rows, :] = own_query
    for a, b in peers:
        copy = remote(
            queries_v.at[p, own_rows],
            queries_v.at[p, own_rows],
            gather_sems,
            a * smp + b,
            me,
            other_p(a),
            other_s(b),
        )
        copy.start()
        sends.append(copy)

    for copy in key_loads:
        copy.wait()
    for a in [0] + steps:
        to_p = other_p(a)
        for b in range(smp):
            if (a, b) != (0, 0):
                to_s = other_s(b)
                there = pl.ds(pl.multiple_of(to_s * piece_rows, piece_rows), piece_rows)
                remote(
                    queries_v.at[to_p, there],
                    queries_v.at[to_p, there],
                    gather_sems,
                    a * smp + b,
                    to_p * smp + to_s,
                    to_p,
                    to_s,
                ).wait_recv()
        g = to_p // pieces_per_kv
        scores = lax.dot_general(
            keys_v[g], queries_v[to_p], by_last, preferred_element_type=jnp.float32
        )
        prefix_scores = scores[:prefix_count]
        suffix_scores = scores[prefix_count:] + bias_v[...]
        top = jnp.maximum(
            jnp.max(prefix_scores, axis=0, keepdims=True),
            jnp.max(suffix_scores, axis=0, keepdims=True),
        )
        weights = jnp.concatenate(
            [
                jnp.exp2((prefix_scores - top) * power_scale).astype(jnp.bfloat16),
                jnp.exp2((suffix_scores - top) * power_scale).astype(jnp.bfloat16),
            ],
            axis=0,
        )
        sums = jnp.dot(flipped_v[g], weights, preferred_element_type=jnp.float32)
        numer_send[to_p] = lax.dot_general(
            eye(lanes),
            sums[:HEAD_WIDTH].astype(jnp.bfloat16),
            by_last,
            preferred_element_type=jnp.float32,
        ).astype(jnp.bfloat16)
        stat_row = lax.broadcasted_iota(jnp.int32, (8, lanes), 0)
        stat_send[to_p] = jnp.where(
            stat_row == 0, top, sums[HEAD_WIDTH : HEAD_WIDTH + 8]
        )
        for b in range(smp):
            to_s = other_s(b)
            there = pl.ds(pl.multiple_of(to_s * piece_rows, piece_rows), piece_rows)
            if (a, b) == (0, 0):
                numer_recv[me] = numer_send[to_p, there, :]
                stat_recv[me] = stat_send[to_p]
            else:
                index = a * smp + b
                for copy in (
                    remote(
                        numer_send.at[to_p, there], numer_recv.at[me], numer_sems, index, me, to_p, to_s
                    ),
                    remote(stat_send.at[to_p], stat_recv.at[me], stat_sems, index, me, to_p, to_s),
                ):
                    copy.start()
                    sends.append(copy)

    new_sum = new_part[p // pieces_per_kv]
    for step in steps:
        source = other_p(step)
        remote(new_part.at[0], new_recv.at[source], new_sems, step, source, source, s).wait_recv()
        new_sum = new_sum + new_recv[source]
    new_key = (new_sum[:, :HEAD_WIDTH] / rms_value).astype(jnp.bfloat16).astype(jnp.float32)
    new_value = (new_sum[:, HEAD_WIDTH:] / rms_value).astype(jnp.bfloat16).astype(jnp.float32)
    own_score = jnp.sum(
        own_query.astype(jnp.float32) * jnp.concatenate([new_key] * piece_heads, axis=0),
        axis=1,
        keepdims=True,
    )
    own_value = jnp.concatenate([new_value] * piece_heads, axis=0)
    for a, b in peers:
        from_p, from_s = other_p(a), other_s(b)
        source = from_p * smp + from_s
        remote(
            numer_send.at[p, own_rows], numer_recv.at[source], numer_sems, a * smp + b, source, from_p, from_s
        ).wait_recv()
        remote(
            stat_send.at[p], stat_recv.at[source], stat_sems, a * smp + b, source, from_p, from_s
        ).wait_recv()
    stats = [stat_recv[i] for i in range(sources)]
    spare = lanes - 8 * sources
    if spare:
        stats.append(jnp.zeros((spare, lanes), jnp.float32))
    column_v[...] = jnp.concatenate(stats, axis=0).T
    columns = column_v[own_rows, :]
    top = own_score
    for i in range(sources):
        top = jnp.maximum(top, columns[:, 8 * i : 8 * i + 1])
    own_weight = jnp.exp2((own_score - top) * power_scale).astype(jnp.bfloat16).astype(jnp.float32)
    factors = jnp.exp2(jnp.minimum(columns - top, 0.0) * power_scale)
    numerator = own_weight * own_value
    denominator = own_weight
    for i in range(sources):
        factor = factors[:, 8 * i : 8 * i + 1]
        numerator = numerator + factor * numer_recv[i].astype(jnp.float32)
        denominator = denominator + factor * columns[:, 8 * i + 1 : 8 * i + 2]
    out_v[p] = (numerator / denominator).astype(jnp.bfloat16)
    for step in steps:
        copy = remote(out_v.at[p], out_v.at[p], out_sems, step, p, other_p(step), s)
        copy.start()
        sends.append(copy)
    for step in steps:
        source = other_p(step)
        remote(out_v.at[p], out_v.at[source], out_sems, step, source, source, s).wait_recv()
    for piece in range(pfx):
        for h in range(piece_heads):
            start = (piece * piece_heads + h) * HEAD_WIDTH
            out_ref[:, start : start + HEAD_WIDTH] = out_v[piece, h * rows : (h + 1) * rows, :]
    for copy in sends:
        copy.wait_send()


def kernel_body(
    pfx,
    smp,
    hidden,
    norm_gain,
    query_weight,
    key_matrix,
    value_matrix,
    prefix_key,
    shared_prefix_value,
    sample_suffix_key,
    sample_suffix_value,
    lengths,
    assign,
):
    rows, width = hidden.shape
    query_cols = query_weight.shape[1]
    kv_cols = key_matrix.shape[1]
    kv_heads = kv_cols // HEAD_WIDTH
    piece_cols = query_cols // pfx
    piece_rows = piece_cols // HEAD_WIDTH * rows
    lanes = smp * piece_rows
    sources = pfx * smp
    suffix_count = rows * sample_suffix_key.shape[1]
    key_count = prefix_key.shape[0] + suffix_count
    wide, narrow = jnp.float32, jnp.bfloat16
    anywhere = pl.BlockSpec(memory_space=pl.ANY)
    scratch = [
        pltpu.VMEM((rows, width), narrow),
        pltpu.VMEM((rows, width), narrow),
        pltpu.VMEM((pfx, width, piece_cols), narrow),
        pltpu.VMEM((2, width, kv_cols), narrow),
        pltpu.VMEM((kv_heads, key_count, HEAD_WIDTH), narrow),
        pltpu.VMEM((kv_heads, key_count, HEAD_WIDTH), narrow),
        pltpu.VMEM((kv_heads, HEAD_WIDTH + 16, key_count), narrow),
        pltpu.VMEM((suffix_count, lanes), wide),
        pltpu.VMEM((pfx, rows, HEAD_WIDTH), wide),
        pltpu.VMEM((pfx, rows, piece_cols), wide),
        pltpu.VMEM((pfx, rows, piece_cols), wide),
        pltpu.VMEM((kv_heads, rows, 2 * HEAD_WIDTH), wide),
        pltpu.VMEM((pfx, rows, 2 * HEAD_WIDTH), wide),
        pltpu.VMEM((pfx, lanes, HEAD_WIDTH), narrow),
        pltpu.VMEM((pfx, lanes, HEAD_WIDTH), narrow),
        pltpu.VMEM((pfx, 8, lanes), wide),
        pltpu.VMEM((sources, piece_rows, HEAD_WIDTH), narrow),
        pltpu.VMEM((sources, 8, lanes), wide),
        pltpu.VMEM((lanes, lanes), wide),
        pltpu.VMEM((pfx, piece_rows, HEAD_WIDTH), narrow),
        pltpu.SemaphoreType.DMA((3 + pfx + 4 * kv_heads,)),
        pltpu.SemaphoreType.DMA((2, pfx)),
        pltpu.SemaphoreType.DMA((2, pfx)),
        pltpu.SemaphoreType.DMA((2, pfx)),
        pltpu.SemaphoreType.DMA((2, sources)),
        pltpu.SemaphoreType.DMA((2, sources)),
        pltpu.SemaphoreType.DMA((2, sources)),
        pltpu.SemaphoreType.DMA((2, pfx)),
    ]
    return pl.pallas_call(
        functools.partial(group_kernel, pfx, smp),
        out_shape=jax.ShapeDtypeStruct((rows, query_cols), narrow),
        in_specs=[anywhere, pl.BlockSpec(memory_space=pltpu.VMEM)]
        + [anywhere] * 7
        + [pl.BlockSpec(memory_space=pltpu.SMEM)] * 2,
        out_specs=pl.BlockSpec(memory_space=pltpu.VMEM),
        scratch_shapes=scratch,
        compiler_params=pltpu.CompilerParams(
            collective_id=0, has_side_effects=True, vmem_limit_bytes=40 * 1024 * 1024
        ),
    )(
        hidden,
        norm_gain.astype(wide).reshape(1, -1),
        query_weight,
        key_matrix,
        value_matrix,
        prefix_key,
        shared_prefix_value,
        sample_suffix_key.reshape(suffix_count, kv_cols),
        sample_suffix_value.reshape(suffix_count, kv_cols),
        lengths,
        assign,
    )


def body(hidden, norm_gain, query_weight, key_matrix, *rest, pfx, smp):
    rows = hidden.shape[0]
    local_heads = query_weight.shape[1] // HEAD_WIDTH
    local_kv = key_matrix.shape[1] // HEAD_WIDTH
    lanes = smp * (local_heads // pfx) * rows
    if local_heads % pfx == 0 and pfx % local_kv == 0 and lanes == 128 and pfx * smp <= 16:
        chosen = functools.partial(kernel_body, pfx, smp)
    else:
        chosen = plain_body
    return chosen(hidden, norm_gain, query_weight, key_matrix, *rest)


def solution(mesh):
    return jax.shard_map(
        functools.partial(body, pfx=mesh.shape["pfx"], smp=mesh.shape["smp"]),
        mesh=mesh,
        in_specs=(
            P(("groups", "smp"), "pfx"),
            P("pfx"),
            P("pfx", "kv"),
            P("pfx", "kv"),
            P("pfx", "kv"),
            P(("groups", "pfx", "smp"), "kv"),
            P(("groups", "pfx", "smp"), "kv"),
            P(("groups", "smp"), "pfx", "kv"),
            P(("groups", "smp"), "pfx", "kv"),
            P(("groups", "smp")),
            P(("groups", "smp")),
        ),
        out_specs=P(("groups", "smp"), "kv"),
        check_vma=False,
    )
```

```python
import functools
import math

import jax
import jax.numpy as jnp
from jax import lax
from jax.experimental import pallas as pl
from jax.experimental.pallas import tpu as pltpu
from jax.sharding import PartitionSpec as P

MODEL_WIDTH = 8192
HEAD_WIDTH = 128


norm_eps = 1e-05
very_negative = -1e30


def prefix_head(operands):
    query_block, key_block, value_block = operands
    scores = jnp.einsum(
        "bgd,kd->bgk", query_block, key_block, preferred_element_type=jnp.float32
    ) * HEAD_WIDTH ** (-0.5)
    top_score = jnp.max(scores, axis=2)
    weights = jnp.exp(scores - top_score[..., None]).astype(jnp.bfloat16)
    denominator = jnp.sum(weights.astype(jnp.float32), axis=2)
    numerator = jnp.einsum("bgk,kd->bgd", weights, value_block, preferred_element_type=jnp.float32)
    return (numerator, denominator, top_score)


def plain_body(
    hidden,
    norm_gain,
    query_weight,
    key_matrix,
    value_matrix,
    prefix_key,
    shared_prefix_value,
    sample_suffix_key,
    sample_suffix_value,
    lengths,
    assign,
):
    local_rows = hidden.shape[0]
    local_kv = key_matrix.shape[1] // HEAD_WIDTH
    local_heads = query_weight.shape[1] // HEAD_WIDTH
    group_width = local_heads // local_kv
    score_scale = HEAD_WIDTH ** (-0.5)
    hidden_wide = hidden.astype(jnp.float32)
    normed = (hidden_wide * norm_gain.astype(jnp.float32)).astype(jnp.bfloat16)
    query_part = jnp.dot(normed, query_weight, preferred_element_type=jnp.float32)
    key_part = jnp.dot(normed, key_matrix, preferred_element_type=jnp.float32)
    value_part = jnp.dot(normed, value_matrix, preferred_element_type=jnp.float32)
    square_part = jnp.sum(hidden_wide * hidden_wide, axis=1)
    query_sum, key_sum, value_sum, square_sum = lax.psum(
        (query_part, key_part, value_part, square_part), "pfx"
    )
    rms_value = jnp.sqrt(square_sum / MODEL_WIDTH + norm_eps)
    query_rows = (query_sum / rms_value[:, None]).astype(jnp.bfloat16)
    new_key = (key_sum / rms_value[:, None]).astype(jnp.bfloat16)
    new_value = (value_sum / rms_value[:, None]).astype(jnp.bfloat16)
    all_queries = lax.all_gather(query_rows, "smp", axis=0, tiled=True)
    sample_count = all_queries.shape[0]
    head_queries = jnp.transpose(
        all_queries.reshape(sample_count, local_kv, group_width, HEAD_WIDTH), (1, 0, 2, 3)
    )
    head_keys = jnp.transpose(prefix_key.reshape(-1, local_kv, HEAD_WIDTH), (1, 0, 2))
    head_values = jnp.transpose(shared_prefix_value.reshape(-1, local_kv, HEAD_WIDTH), (1, 0, 2))
    pre_numer, pre_denom, pre_top = lax.map(prefix_head, (head_queries, head_keys, head_values))
    pre_numer = jnp.transpose(pre_numer, (1, 0, 2, 3)).reshape(
        sample_count, local_heads, HEAD_WIDTH
    )
    pre_denom = jnp.transpose(pre_denom, (1, 0, 2)).reshape(sample_count, local_heads)
    pre_top = jnp.transpose(pre_top, (1, 0, 2)).reshape(sample_count, local_heads)
    row_base = lax.axis_index("smp") * local_rows
    slot_index = assign - row_base
    one_hot = (slot_index[:, None] == jnp.arange(local_rows, dtype=jnp.int32)[None, :]).astype(
        jnp.float32
    )
    slot_query = jnp.einsum(
        "rs,rx->sx", one_hot, query_rows.astype(jnp.float32), precision=lax.Precision.HIGHEST
    ).astype(jnp.bfloat16)
    slot_query = slot_query.reshape(local_rows, local_kv, group_width, HEAD_WIDTH)
    suffix_len = sample_suffix_key.shape[1]
    suffix_keys = sample_suffix_key.reshape(local_rows, suffix_len, local_kv, HEAD_WIDTH)
    suffix_values = sample_suffix_value.reshape(local_rows, suffix_len, local_kv, HEAD_WIDTH)
    suffix_scores = (
        jnp.einsum("shgd,sthd->shgt", slot_query, suffix_keys, preferred_element_type=jnp.float32)
        * score_scale
    )
    position = lax.axis_index("pfx") * suffix_len + jnp.arange(suffix_len, dtype=jnp.int32)
    live_mask = (position[None, :] < lengths[:, None])[:, None, None, :]
    suffix_scores = jnp.where(live_mask, suffix_scores, very_negative)
    suffix_top = jnp.max(suffix_scores, axis=3)
    suffix_weights = jnp.where(
        live_mask, jnp.exp(suffix_scores - suffix_top[..., None]), 0.0
    ).astype(jnp.bfloat16)
    suffix_denom = jnp.sum(suffix_weights.astype(jnp.float32), axis=3)
    suffix_numer = jnp.einsum(
        "shgt,sthd->shgd", suffix_weights, suffix_values, preferred_element_type=jnp.float32
    )
    row_numer = jnp.einsum(
        "rs,shgd->rhgd", one_hot, suffix_numer, precision=lax.Precision.HIGHEST
    ).reshape(local_rows, local_heads, HEAD_WIDTH)
    row_denom = jnp.einsum(
        "rs,shg->rhg", one_hot, suffix_denom, precision=lax.Precision.HIGHEST
    ).reshape(local_rows, local_heads)
    row_top = jnp.einsum(
        "rs,shg->rhg", one_hot, suffix_top, precision=lax.Precision.HIGHEST
    ).reshape(local_rows, local_heads)
    full_top = lax.dynamic_update_slice(
        jnp.full((sample_count, local_heads), very_negative, jnp.float32), row_top, (row_base, 0)
    )
    local_top = jnp.maximum(pre_top, full_top)
    global_top = lax.pmax(local_top, ("pfx", "smp"))
    own_top = lax.dynamic_slice_in_dim(global_top, row_base, local_rows, 0)
    pre_factor = jnp.exp(pre_top - global_top)
    row_factor = jnp.exp(row_top - own_top)
    scaled_row_numer = row_numer * row_factor[..., None]
    scaled_row_denom = row_denom * row_factor
    term_numer = pre_numer * pre_factor[..., None]
    term_denom = pre_denom * pre_factor
    term_numer = lax.dynamic_update_slice(
        term_numer,
        lax.dynamic_slice_in_dim(term_numer, row_base, local_rows, 0) + scaled_row_numer,
        (row_base, 0, 0),
    )
    term_denom = lax.dynamic_update_slice(
        term_denom,
        lax.dynamic_slice_in_dim(term_denom, row_base, local_rows, 0) + scaled_row_denom,
        (row_base, 0),
    )
    block_numer, block_denom = (
        lax.psum_scatter(
            term_numer.astype(jnp.bfloat16), "smp", scatter_dimension=0, tiled=True
        ).astype(jnp.float32),
        lax.psum_scatter(
            term_denom.astype(jnp.bfloat16), "smp", scatter_dimension=0, tiled=True
        ).astype(jnp.float32),
    )
    numerator, denominator = (
        lax.psum(block_numer.astype(jnp.bfloat16), "pfx").astype(jnp.float32),
        lax.psum(block_denom.astype(jnp.bfloat16), "pfx").astype(jnp.float32),
    )
    query_wide = query_rows.reshape(local_rows, local_kv, group_width, HEAD_WIDTH).astype(
        jnp.float32
    )
    own_key = new_key.reshape(local_rows, local_kv, 1, HEAD_WIDTH).astype(jnp.float32)
    own_score = (jnp.sum(query_wide * own_key, axis=3) * score_scale).reshape(
        local_rows, local_heads
    )
    final_top = jnp.maximum(own_top, own_score)
    old_factor = jnp.exp(own_top - final_top)
    own_weight = lax.optimization_barrier(
        jnp.exp(own_score - final_top).astype(jnp.bfloat16)
    ).astype(jnp.float32)
    own_value = jnp.broadcast_to(
        new_value.reshape(local_rows, local_kv, 1, HEAD_WIDTH).astype(jnp.float32),
        (local_rows, local_kv, group_width, HEAD_WIDTH),
    ).reshape(local_rows, local_heads, HEAD_WIDTH)
    numerator = numerator * old_factor[..., None] + own_weight[..., None] * own_value
    denominator = denominator * old_factor + own_weight
    return (
        (numerator / denominator[..., None])
        .astype(jnp.bfloat16)
        .reshape(local_rows, local_heads * HEAD_WIDTH)
    )


def group_kernel(
    pfx,
    smp,
    hidden_hbm,
    gain_ref,
    query_weight_hbm,
    key_matrix_hbm,
    value_matrix_hbm,
    prefix_key_hbm,
    prefix_value_hbm,
    suffix_key_hbm,
    suffix_value_hbm,
    lengths_ref,
    assign_ref,
    out_ref,
    hidden_v,
    normed_v,
    query_weight_v,
    new_weight_v,
    keys_v,
    values_v,
    flipped_v,
    bias_v,
    square_v,
    query_part,
    query_recv,
    new_part,
    new_recv,
    queries_v,
    numer_send,
    stat_send,
    numer_recv,
    stat_recv,
    column_v,
    out_v,
    load_sem,
    square_sems,
    query_sems,
    new_sems,
    gather_sems,
    numer_sems,
    stat_sems,
    out_sems,
):
    rows, width = hidden_v.shape
    kv_heads, key_count, _ = keys_v.shape
    prefix_count = prefix_key_hbm.shape[0]
    suffix_count = suffix_key_hbm.shape[0]
    suffix_len = suffix_count // rows
    piece_cols = query_weight_v.shape[2]
    piece_heads = piece_cols // HEAD_WIDTH
    piece_rows = piece_heads * rows
    lanes = smp * piece_rows
    pieces_per_kv = pfx // kv_heads
    sources = pfx * smp
    power_scale = HEAD_WIDTH ** (-0.5) * math.log2(math.e)

    p = lax.axis_index("pfx")
    s = lax.axis_index("smp")
    me = p * smp + s

    def other_p(step):
        partner, bit = p, 1
        while bit < pfx:
            if step & bit:
                partner = partner + bit - 2 * bit * lax.rem(p // bit, 2)
            bit *= 2
        return partner

    def other_s(step):
        return lax.rem(s + step, smp)

    steps = list(range(1, pfx))
    order = [step for step in steps if step > 1] + [1, 0]
    peers = [(a, b) for a in [0] + steps for b in range(smp) if (a, b) != (0, 0)]

    def remote(source, target, sems, send_index, recv_index, to_p, to_s):
        return pltpu.make_async_remote_copy(
            src_ref=source,
            dst_ref=target,
            send_sem=sems.at[0, send_index],
            recv_sem=sems.at[1, recv_index],
            device_id={"pfx": to_p, "smp": to_s},
            device_id_type=pl.DeviceIdType.MESH,
        )

    loads = []

    def load(source, target):
        copy = pltpu.make_async_copy(source, target, load_sem.at[len(loads)])
        copy.start()
        loads.append(copy)
        return copy

    hidden_load = load(hidden_hbm, hidden_v)
    query_loads = []
    for slot, step in enumerate(order):
        start = pl.multiple_of(other_p(step) * piece_cols, piece_cols)
        query_loads.append(
            load(query_weight_hbm.at[:, pl.ds(start, piece_cols)], query_weight_v.at[slot])
        )
    new_loads = [
        load(key_matrix_hbm, new_weight_v.at[0]),
        load(value_matrix_hbm, new_weight_v.at[1]),
    ]
    value_loads, key_loads = [], []
    for g in range(kv_heads):
        head = pl.ds(g * HEAD_WIDTH, HEAD_WIDTH)
        early, late = pl.ds(0, prefix_count), pl.ds(prefix_count, suffix_count)
        value_loads.append(load(prefix_value_hbm.at[:, head], values_v.at[g, early]))
        value_loads.append(load(suffix_value_hbm.at[:, head], values_v.at[g, late]))
        key_loads.append(load(prefix_key_hbm.at[:, head], keys_v.at[g, early]))
        key_loads.append(load(suffix_key_hbm.at[:, head], keys_v.at[g, late]))

    barrier = pltpu.get_barrier_semaphore()
    for a, b in peers:
        pl.semaphore_signal(
            barrier,
            inc=1,
            device_id={"pfx": other_p(a), "smp": other_s(b)},
            device_id_type=pl.DeviceIdType.MESH,
        )

    hidden_load.wait()
    hidden_wide = hidden_v[...].astype(jnp.float32)
    normed_v[...] = (hidden_wide * gain_ref[...].astype(jnp.float32).reshape(1, width)).astype(jnp.bfloat16)
    square_part = jnp.sum(hidden_wide * hidden_wide, axis=1, keepdims=True)
    square_v[p] = jnp.broadcast_to(square_part, (rows, HEAD_WIDTH))
    pl.semaphore_wait(barrier, len(peers))

    sends = []
    for step in steps:
        copy = remote(square_v.at[p], square_v.at[p], square_sems, step, p, other_p(step), s)
        copy.start()
        sends.append(copy)

    for slot, step in enumerate(order):
        query_loads[slot].wait()
        query_part[slot] = jnp.dot(
            normed_v[...], query_weight_v[slot], preferred_element_type=jnp.float32
        )
        if step:
            copy = remote(
                query_part.at[slot], query_recv.at[p], query_sems, step, p, other_p(step), s
            )
            copy.start()
            sends.append(copy)
    for which in range(2):
        new_loads[which].wait()
        product = jnp.dot(
            normed_v[...], new_weight_v[which], preferred_element_type=jnp.float32
        )
        for g in range(kv_heads):
            new_part[g, :, which * HEAD_WIDTH : (which + 1) * HEAD_WIDTH] = product[
                :, g * HEAD_WIDTH : (g + 1) * HEAD_WIDTH
            ]
    for step in steps:
        copy = remote(
            new_part.at[other_p(step) // pieces_per_kv],
            new_recv.at[p],
            new_sems,
            step,
            p,
            other_p(step),
            s,
        )
        copy.start()
        sends.append(copy)

    ones = jnp.ones((flipped_v.shape[1] - HEAD_WIDTH, key_count), jnp.bfloat16)

    def eye(size):
        return (
            lax.broadcasted_iota(jnp.int32, (size, size), 0)
            == lax.broadcasted_iota(jnp.int32, (size, size), 1)
        ).astype(jnp.bfloat16)

    by_last = (((1,), (1,)), ((), ()))
    for copy in value_loads:
        copy.wait()
    for g in range(kv_heads):
        flipped_v[g, :HEAD_WIDTH, :] = lax.dot_general(
            eye(HEAD_WIDTH), values_v[g], by_last, preferred_element_type=jnp.float32
        ).astype(jnp.bfloat16)
        flipped_v[g, HEAD_WIDTH:, :] = ones
    lane = lax.broadcasted_iota(jnp.int32, (suffix_len, lanes), 1)
    position = lax.broadcasted_iota(jnp.int32, (suffix_len, lanes), 0) + p * suffix_len
    lane_row = lax.rem(lane, rows)
    lane_sample = jnp.full((suffix_len, lanes), -1, jnp.int32)
    for row in range(rows):
        lane_sample = jnp.where(lane_row == row, assign_ref[row] - s * rows, lane_sample)
    own_lane = (lane >= s * piece_rows) & (lane < (s + 1) * piece_rows)
    lane_sample = jnp.where(own_lane, lane_sample, -1)
    for sample in range(rows):
        live = (lane_sample == sample) & (position < lengths_ref[sample])
        bias_v[sample * suffix_len : (sample + 1) * suffix_len, :] = jnp.where(
            live, 0.0, very_negative
        )

    square_sum = square_v[p]
    query_sum = query_part[order.index(0)]
    for step in steps:
        source = other_p(step)
        remote(square_v.at[p], square_v.at[source], square_sems, step, source, source, s).wait_recv()
        remote(
            query_part.at[0], query_recv.at[source], query_sems, step, source, source, s
        ).wait_recv()
        square_sum = square_sum + square_v[source]
        query_sum = query_sum + query_recv[source]
    rms_value = jnp.sqrt(square_sum / (width * pfx) + norm_eps)
    own_rows = pl.ds(pl.multiple_of(s * piece_rows, piece_rows), piece_rows)
    own_query = jnp.concatenate(
        [
            query_sum[:, h * HEAD_WIDTH : (h + 1) * HEAD_WIDTH] / rms_value
            for h in range(piece_heads)
        ],
        axis=0,
    ).astype(jnp.bfloat16)
    queries_v[p, own_rows, :] = own_query
    for a, b in peers:
        copy = remote(
            queries_v.at[p, own_rows],
            queries_v.at[p, own_rows],
            gather_sems,
            a * smp + b,
            me,
            other_p(a),
            other_s(b),
        )
        copy.start()
        sends.append(copy)

    for copy in key_loads:
        copy.wait()
    for a in [0] + steps:
        to_p = other_p(a)
        for b in range(smp):
            if (a, b) != (0, 0):
                to_s = other_s(b)
                there = pl.ds(pl.multiple_of(to_s * piece_rows, piece_rows), piece_rows)
                remote(
                    queries_v.at[to_p, there],
                    queries_v.at[to_p, there],
                    gather_sems,
                    a * smp + b,
                    to_p * smp + to_s,
                    to_p,
                    to_s,
                ).wait_recv()
        g = to_p // pieces_per_kv
        scores = lax.dot_general(
            keys_v[g], queries_v[to_p], by_last, preferred_element_type=jnp.float32
        )
        prefix_scores = scores[:prefix_count]
        suffix_scores = scores[prefix_count:] + bias_v[...]
        top = jnp.maximum(
            jnp.max(prefix_scores, axis=0, keepdims=True),
            jnp.max(suffix_scores, axis=0, keepdims=True),
        )
        weights = jnp.concatenate(
            [
                jnp.exp2((prefix_scores - top) * power_scale).astype(jnp.bfloat16),
                jnp.exp2((suffix_scores - top) * power_scale).astype(jnp.bfloat16),
            ],
            axis=0,
        )
        sums = jnp.dot(flipped_v[g], weights, preferred_element_type=jnp.float32)
        numer_send[to_p] = lax.dot_general(
            eye(lanes),
            sums[:HEAD_WIDTH].astype(jnp.bfloat16),
            by_last,
            preferred_element_type=jnp.float32,
        ).astype(jnp.bfloat16)
        stat_row = lax.broadcasted_iota(jnp.int32, (8, lanes), 0)
        stat_send[to_p] = jnp.where(
            stat_row == 0, top, sums[HEAD_WIDTH : HEAD_WIDTH + 8]
        )
        for b in range(smp):
            to_s = other_s(b)
            there = pl.ds(pl.multiple_of(to_s * piece_rows, piece_rows), piece_rows)
            if (a, b) == (0, 0):
                numer_recv[me] = numer_send[to_p, there, :]
                stat_recv[me] = stat_send[to_p]
            else:
                index = a * smp + b
                for copy in (
                    remote(
                        numer_send.at[to_p, there], numer_recv.at[me], numer_sems, index, me, to_p, to_s
                    ),
                    remote(stat_send.at[to_p], stat_recv.at[me], stat_sems, index, me, to_p, to_s),
                ):
                    copy.start()
                    sends.append(copy)

    new_sum = new_part[p // pieces_per_kv]
    for step in steps:
        source = other_p(step)
        remote(new_part.at[0], new_recv.at[source], new_sems, step, source, source, s).wait_recv()
        new_sum = new_sum + new_recv[source]
    new_key = (new_sum[:, :HEAD_WIDTH] / rms_value).astype(jnp.bfloat16).astype(jnp.float32)
    new_value = (new_sum[:, HEAD_WIDTH:] / rms_value).astype(jnp.bfloat16).astype(jnp.float32)
    own_score = jnp.sum(
        own_query.astype(jnp.float32) * jnp.concatenate([new_key] * piece_heads, axis=0),
        axis=1,
        keepdims=True,
    )
    own_value = jnp.concatenate([new_value] * piece_heads, axis=0)
    for a, b in peers:
        from_p, from_s = other_p(a), other_s(b)
        source = from_p * smp + from_s
        remote(
            numer_send.at[p, own_rows], numer_recv.at[source], numer_sems, a * smp + b, source, from_p, from_s
        ).wait_recv()
        remote(
            stat_send.at[p], stat_recv.at[source], stat_sems, a * smp + b, source, from_p, from_s
        ).wait_recv()
    stats = [stat_recv[i] for i in range(sources)]
    spare = lanes - 8 * sources
    if spare:
        stats.append(jnp.zeros((spare, lanes), jnp.float32))
    column_v[...] = jnp.concatenate(stats, axis=0).T
    columns = column_v[own_rows, :]
    top = own_score
    for i in range(sources):
        top = jnp.maximum(top, columns[:, 8 * i : 8 * i + 1])
    own_weight = jnp.exp2((own_score - top) * power_scale).astype(jnp.bfloat16).astype(jnp.float32)
    factors = jnp.exp2(jnp.minimum(columns - top, 0.0) * power_scale)
    numerator = own_weight * own_value
    denominator = own_weight
    for i in range(sources):
        factor = factors[:, 8 * i : 8 * i + 1]
        numerator = numerator + factor * numer_recv[i].astype(jnp.float32)
        denominator = denominator + factor * columns[:, 8 * i + 1 : 8 * i + 2]
    out_v[p] = (numerator / denominator).astype(jnp.bfloat16)
    for step in steps:
        copy = remote(out_v.at[p], out_v.at[p], out_sems, step, p, other_p(step), s)
        copy.start()
        sends.append(copy)
    for step in steps:
        source = other_p(step)
        remote(out_v.at[p], out_v.at[source], out_sems, step, source, source, s).wait_recv()
    for piece in range(pfx):
        for h in range(piece_heads):
            start = (piece * piece_heads + h) * HEAD_WIDTH
            out_ref[:, start : start + HEAD_WIDTH] = out_v[piece, h * rows : (h + 1) * rows, :]
    for copy in sends:
        copy.wait_send()


def kernel_body(
    pfx,
    smp,
    hidden,
    norm_gain,
    query_weight,
    key_matrix,
    value_matrix,
    prefix_key,
    shared_prefix_value,
    sample_suffix_key,
    sample_suffix_value,
    lengths,
    assign,
):
    rows, width = hidden.shape
    query_cols = query_weight.shape[1]
    kv_cols = key_matrix.shape[1]
    kv_heads = kv_cols // HEAD_WIDTH
    piece_cols = query_cols // pfx
    piece_rows = piece_cols // HEAD_WIDTH * rows
    lanes = smp * piece_rows
    sources = pfx * smp
    suffix_count = rows * sample_suffix_key.shape[1]
    key_count = prefix_key.shape[0] + suffix_count
    wide, narrow = jnp.float32, jnp.bfloat16
    anywhere = pl.BlockSpec(memory_space=pltpu.HBM)
    scratch = [
        pltpu.VMEM((rows, width), narrow),
        pltpu.VMEM((rows, width), narrow),
        pltpu.VMEM((pfx, width, piece_cols), narrow),
        pltpu.VMEM((2, width, kv_cols), narrow),
        pltpu.VMEM((kv_heads, key_count, HEAD_WIDTH), narrow),
        pltpu.VMEM((kv_heads, key_count, HEAD_WIDTH), narrow),
        pltpu.VMEM((kv_heads, HEAD_WIDTH + 16, key_count), narrow),
        pltpu.VMEM((suffix_count, lanes), wide),
        pltpu.VMEM((pfx, rows, HEAD_WIDTH), wide),
        pltpu.VMEM((pfx, rows, piece_cols), wide),
        pltpu.VMEM((pfx, rows, piece_cols), wide),
        pltpu.VMEM((kv_heads, rows, 2 * HEAD_WIDTH), wide),
        pltpu.VMEM((pfx, rows, 2 * HEAD_WIDTH), wide),
        pltpu.VMEM((pfx, lanes, HEAD_WIDTH), narrow),
        pltpu.VMEM((pfx, lanes, HEAD_WIDTH), narrow),
        pltpu.VMEM((pfx, 8, lanes), wide),
        pltpu.VMEM((sources, piece_rows, HEAD_WIDTH), narrow),
        pltpu.VMEM((sources, 8, lanes), wide),
        pltpu.VMEM((lanes, lanes), wide),
        pltpu.VMEM((pfx, piece_rows, HEAD_WIDTH), narrow),
        pltpu.SemaphoreType.DMA((3 + pfx + 4 * kv_heads,)),
        pltpu.SemaphoreType.DMA((2, pfx)),
        pltpu.SemaphoreType.DMA((2, pfx)),
        pltpu.SemaphoreType.DMA((2, pfx)),
        pltpu.SemaphoreType.DMA((2, sources)),
        pltpu.SemaphoreType.DMA((2, sources)),
        pltpu.SemaphoreType.DMA((2, sources)),
        pltpu.SemaphoreType.DMA((2, pfx)),
    ]
    return pl.pallas_call(
        functools.partial(group_kernel, pfx, smp),
        out_shape=jax.ShapeDtypeStruct((rows, query_cols), narrow),
        in_specs=[anywhere, pl.BlockSpec(memory_space=pltpu.VMEM)]
        + [anywhere] * 7
        + [pl.BlockSpec(memory_space=pltpu.SMEM)] * 2,
        out_specs=pl.BlockSpec(memory_space=pltpu.VMEM),
        scratch_shapes=scratch,
        compiler_params=pltpu.CompilerParams(
            collective_id=0, has_side_effects=True, vmem_limit_bytes=56 * 1024 * 1024
        ),
    )(
        hidden,
        norm_gain,
        query_weight,
        key_matrix,
        value_matrix,
        prefix_key,
        shared_prefix_value,
        sample_suffix_key.reshape(suffix_count, kv_cols),
        sample_suffix_value.reshape(suffix_count, kv_cols),
        lengths,
        assign,
    )


def body(hidden, norm_gain, query_weight, key_matrix, *rest, pfx, smp):
    rows = hidden.shape[0]
    local_heads = query_weight.shape[1] // HEAD_WIDTH
    local_kv = key_matrix.shape[1] // HEAD_WIDTH
    lanes = smp * (local_heads // pfx) * rows
    whole = local_heads % pfx == 0 and pfx % local_kv == 0 and pfx & (pfx - 1) == 0
    if whole and lanes == 128 and 8 * pfx * smp <= lanes:
        chosen = functools.partial(kernel_body, pfx, smp)
    else:
        chosen = plain_body
    return chosen(hidden, norm_gain, query_weight, key_matrix, *rest)


def solution(mesh):
    return jax.shard_map(
        functools.partial(body, pfx=mesh.shape["pfx"], smp=mesh.shape["smp"]),
        mesh=mesh,
        in_specs=(
            P(("groups", "smp"), "pfx"),
            P("pfx"),
            P("pfx", "kv"),
            P("pfx", "kv"),
            P("pfx", "kv"),
            P(("groups", "pfx", "smp"), "kv"),
            P(("groups", "pfx", "smp"), "kv"),
            P(("groups", "smp"), "pfx", "kv"),
            P(("groups", "smp"), "pfx", "kv"),
            P(("groups", "smp")),
            P(("groups", "smp")),
        ),
        out_specs=P(("groups", "smp"), "kv"),
        check_vma=False,
    )
```
